512 devices in a mesh: dp: 32 (over x, z_lo), expert: 16 (over y, z_hi, core).
Axes of the slice: x: 4, y: 4, z: 16 (z_hi: 2, z_lo: 8; z = z_hi * 8 + z_lo), core: 2. Of those that a mesh axis runs over, the one named last changes fastest.
Arguments:
- grads: bfloat16 [262144, 768], P(('dp', 'expert'))
- block_expert: int32 [8192], P(('dp', 'expert')), may hold values from 0 to 15, as said below
- grad_weight: bfloat16 [16, 4096, 768], P('expert', 'dp'), may hold values from -1.1953125 to 1.1953125
- damping: float32 [16], P('expert'), may hold values from 0.1 to 1
Outputs:
- preconditioned: float32 [16, 4096, 768], P('expert', 'dp')
The draws below stay inside these ranges and needn't reach their ends.
Inputs may be any that keep to these rules, and one draw needn't show every extreme that they name: `block_expert`: among the 16 blocks of one device no expert appears more than 2 times; in every draw one expert appears exactly 2 times on every device.
All inputs are finite; a program needn't handle non-finite values.
Results may differ from the reference program's by a relative error of at most 0.0003.
Values may be sent and summed in bfloat16 or wider, within the bound.
No kernel may reach another device: no remote copies, remote signals or barrier semaphores. Data moves between devices by JAX's collectives and lax.ppermute only.
A program may use at most 128 MiB of HBM per device.

```python
import math
import jax
import jax.numpy as jnp
from jax import lax

D = 4096
FF = 768
TB = 32
EXPERTS = 16
BLOCKS_DEV = 16
TOKENS = 262144
CAPE = 2
N_DP = 32
N_EXPERT = 16


def draw_grads(key, part):
    key = jax.random.fold_in(key, 23)
    key_base, key_rows, key_cols = jax.random.split(key, 3)
    base = jax.random.normal(key_base, (TOKENS, FF), jnp.float32)
    rows = jnp.exp(jax.random.uniform(key_rows, (TOKENS, 1), jnp.float32, math.log(0.3), math.log(3.0)))
    cols = jnp.exp(jax.random.uniform(key_cols, (1, FF), jnp.float32, math.log(0.3), math.log(3.0)))
    value = base * rows * cols
    return value.astype(jnp.bfloat16)


def draw_block_expert(key, part):
    key = jax.random.fold_in(key, 11)
    key_hot, key_rest = jax.random.split(key)
    hottest = jax.random.randint(key_hot, (), 0, EXPERTS)
    others = (hottest + 1 + jnp.arange(EXPERTS - 1, dtype=jnp.int32)) % EXPERTS
    supply = jnp.tile(others, CAPE)

    def one_device(device_key):
        key_pick, key_order = jax.random.split(device_key)
        picked = jax.random.permutation(key_pick, supply)[:BLOCKS_DEV - CAPE]
        together = jnp.concatenate([jnp.zeros((CAPE,), jnp.int32) + hottest, picked])
        return jax.random.permutation(key_order, together)
    device_keys = jax.random.split(key_rest, N_DP * N_EXPERT)
    return jax.vmap(one_device)(device_keys).reshape(-1).astype(jnp.int32)


def steps_of(key, extent, cuts, smallest, largest):
    loudness = 1.0
    for axis_at, shards_of in cuts:
        heights = jax.random.uniform(jax.random.fold_in(jax.random.fold_in(key, 6), axis_at), (shards_of,), jnp.float32, smallest / len(cuts), largest / len(cuts))
        loudness = loudness * jnp.repeat(jnp.exp(heights), extent[axis_at] // shards_of).reshape((-1,) + (1,) * (len(extent) - 1 - axis_at))
    return loudness


def bell_draw(own_key, extent, deviation, limit, cuts=(), kind=jnp.bfloat16):
    loudness = steps_of(own_key, extent, cuts, -0.22, 0.18) if cuts else 1.0
    drawn = jax.random.normal(own_key, extent, jnp.float32) * deviation * loudness
    return jnp.minimum(jnp.maximum(drawn, -limit), limit).astype(kind)


def setup_inputs(seed: int = 0) -> dict:
    keys = jax.random.split(jax.random.key(seed), 5)
    return {
        "grads": draw_grads(jax.random.fold_in(keys[4], 71), 0),
        "block_expert": draw_block_expert(jax.random.fold_in(keys[4], 71), 0),
        "grad_weight": bell_draw(keys[2], (EXPERTS, D, FF), 0.2, 1.1953125, ((0, 16), (1, 32))),
        "damping": jnp.clip(jnp.exp(math.log(1.0) - 2.3025851 * jax.random.uniform(keys[3], (EXPERTS,), jnp.float32) ** steps_of(keys[3], (EXPERTS,), ((0, 16),), -0.2, 0.2)), 0.1, 1.0),
    }


def inverse_of(matrix):
    lower = jnp.linalg.cholesky(matrix)
    identity = jnp.eye(matrix.shape[0], dtype=jnp.float32)
    lower_inv = jax.scipy.linalg.solve_triangular(lower, identity, lower=True)
    return jnp.dot(lower_inv.T, lower_inv, precision=lax.Precision.HIGHEST)

def reference(grads, block_expert, grad_weight, damping):
    pieces = grads.reshape(-1, TB, FF)

    def accumulate(carry, item):
        piece, which = item
        term = jnp.dot(piece.T.astype(jnp.float32), piece.astype(jnp.float32), preferred_element_type=jnp.float32)
        current = lax.dynamic_index_in_dim(carry, which, 0, keepdims=False)
        carry = lax.dynamic_update_index_in_dim(carry, current + term, which, 0)
        return (carry, None)
    start = jnp.zeros((EXPERTS, FF, FF), jnp.float32)
    grams, _ = lax.scan(accumulate, start, (pieces, block_expert.astype(jnp.int32)))
    scale = EXPERTS / TOKENS
    identity = jnp.eye(FF, dtype=jnp.float32)

    def apply_one(item):
        gram, weight, damp = item
        matrix = gram * scale + damp * identity
        inverse = inverse_of(matrix)
        return jnp.dot(weight.astype(jnp.float32), inverse, precision=lax.Precision.HIGHEST)
    return lax.map(apply_one, (grams, grad_weight, damping))
```

```python
import functools

import jax
import jax.numpy as jnp
from jax import lax
from jax.experimental import pallas as pl
from jax.experimental.pallas import tpu as pltpu
from jax.sharding import Mesh
from jax.sharding import PartitionSpec as P

FB = 128
FF = 768
NB = FF // FB
TRI = NB * (NB + 1) // 2
CAP = 2
CHUNK = 48
ROWS = 64 * CHUNK
BF16 = jnp.bfloat16
F32 = jnp.float32


def product(left, right):
    return jnp.dot(left, right, precision=lax.Precision.HIGHEST)


def tri_index(row_block, col_block):
    return row_block * (row_block + 1) // 2 + col_block


def lower_inverse_blocks(packed, scale, damp):
    identity = jnp.eye(FB, dtype=F32)

    def entry(row_block, col_block):
        value = packed[tri_index(row_block, col_block)] * scale
        if row_block == col_block:
            value = value + damp * identity
        return value

    lower = {}
    diag_inv = {}
    for step in range(NB):
        acc = entry(step, step)
        for other in range(step):
            acc = acc - product(lower[step, other], lower[step, other].T)
        lower[step, step] = jnp.linalg.cholesky(acc)
        diag_inv[step] = jax.scipy.linalg.solve_triangular(lower[step, step], identity, lower=True)
        for row_block in range(step + 1, NB):
            acc = entry(row_block, step)
            for other in range(step):
                acc = acc - product(lower[row_block, other], lower[step, other].T)
            lower[row_block, step] = product(acc, diag_inv[step].T)
    inverse_blocks = {}
    for col_block in range(NB):
        inverse_blocks[col_block, col_block] = diag_inv[col_block]
        for row_block in range(col_block + 1, NB):
            total = jnp.zeros((FB, FB), F32)
            for other in range(col_block, row_block):
                total = total + product(lower[row_block, other], inverse_blocks[other, col_block])
            inverse_blocks[row_block, col_block] = -product(diag_inv[row_block], total)
    return inverse_blocks


def direct_apply(packed, weight, scale, damp):
    blocks = lower_inverse_blocks(packed, scale, damp)
    rows = []
    for upper in range(NB):
        pieces = [
            blocks[upper, low] if low <= upper else jnp.zeros((FB, FB), F32) for low in range(NB)
        ]
        rows.append(jnp.concatenate(pieces, axis=1))
    lower_inv = jnp.concatenate(rows, axis=0)
    return product(weight.astype(F32), product(lower_inv.T, lower_inv))


def dot32(left, right):
    return jnp.dot(left, right, preferred_element_type=F32)


def split(value):
    high = value.astype(BF16)
    return high, (value - high.astype(F32)).astype(BF16)


def solve_kernel(scale, damp_ref, packed_ref, weight_ref, out_ref, ok_ref,
                 fh, fl, r1, r2, r4, r8, bvec, xvec):
    damp = damp_ref[0]
    row_id = lax.broadcasted_iota(jnp.int32, (FB, FB), 0)
    col_id = lax.broadcasted_iota(jnp.int32, (FB, FB), 1)
    eye = jnp.where(row_id == col_id, 1.0, 0.0).astype(F32)

    s_row, s_col = [], []
    for i in range(NB):
        t = tri_index(i, i)
        dia = packed_ref[t * FB:(t + 1) * FB, :] * eye
        s_row.append(lax.rsqrt(jnp.sum(dia, axis=0, keepdims=True) * scale + damp))
        s_col.append(lax.rsqrt(jnp.sum(dia, axis=1, keepdims=True) * scale + damp))
    norm = jnp.zeros((FB, FB), F32)
    for i in range(NB):
        for j in range(i + 1):
            t = tri_index(i, j)
            block = packed_ref[t * FB:(t + 1) * FB, :] * scale
            if i == j:
                block = block + damp * eye
            block = block * s_col[i] * s_row[j]
            norm = norm + block * block * (1.0 if i == j else 2.0)
            high, low = split(block)
            fh[i * FB:(i + 1) * FB, j * FB:(j + 1) * FB] = high
            fl[i * FB:(i + 1) * FB, j * FB:(j + 1) * FB] = low
            if i != j:
                turned = block.T
                high, low = split(turned)
                fh[j * FB:(j + 1) * FB, i * FB:(i + 1) * FB] = high
                fl[j * FB:(j + 1) * FB, i * FB:(i + 1) * FB] = low
    total = jnp.sum(jnp.sum(norm, axis=0, keepdims=True), axis=1, keepdims=True)
    alpha = float(FF) / total
    for i in range(NB):
        rows = slice(i * FB, (i + 1) * FB)
        for j in range(NB):
            cols = slice(j * FB, (j + 1) * FB)
            part = fh[rows, cols].astype(F32) + fl[rows, cols].astype(F32)
            value = -alpha * part
            if i == j:
                value = value + eye
            r1[rows, cols] = value.astype(BF16)
    for i in range(NB):
        rows = slice(i * FB, (i + 1) * FB)
        r2[rows, :] = dot32(r1[rows, :], r1[...]).astype(BF16)
    for i in range(NB):
        rows = slice(i * FB, (i + 1) * FB)
        r4[rows, :] = dot32(r2[rows, :], r2[...]).astype(BF16)
    power = jnp.zeros((1, FF), F32)
    for i in range(NB):
        rows = slice(i * FB, (i + 1) * FB)
        value = dot32(r4[rows, :], r4[...])
        power = power + jnp.sum(value * value, axis=0, keepdims=True)
        r8[rows, :] = value.astype(BF16)
    power = jnp.sum(power, axis=1, keepdims=True)

    scales = jnp.concatenate(s_row, axis=1)
    bvec[...] = weight_ref[...].astype(F32) * scales

    def near_inverse(value):
        value = value + dot32(value.astype(BF16), r8[...])
        value = value + dot32(value.astype(BF16), r4[...])
        value = value + dot32(value.astype(BF16), r2[...])
        value = value + dot32(value.astype(BF16), r1[...])
        return value * alpha

    def residual(value):
        high, low = split(value)
        return bvec[...] - (
            dot32(high, fh[...]) + (dot32(low, fh[...]) + dot32(high, fl[...]))
        )

    xvec[...] = near_inverse(bvec[...])
    xvec[...] = xvec[...] + near_inverse(residual(xvec[...]))
    left = residual(xvec[...])
    left_norm = jnp.sum(left * left, axis=1, keepdims=True)
    b_norm = jnp.sum(bvec[...] * bvec[...], axis=1, keepdims=True)
    out_ref[...] = (xvec[...] + near_inverse(left)) * scales
    bad = jnp.sum(jnp.where(left_norm <= 1e-6 * b_norm, 0.0, 1.0), axis=0, keepdims=True)
    bad = bad + jnp.where(power <= 0.25, 0.0, 1.0)
    ok_ref[...] = jnp.broadcast_to(bad, (8, 128))


def refined_apply(packed, weight, scale, damp):
    return pl.pallas_call(
        functools.partial(solve_kernel, scale),
        out_shape=(
            jax.ShapeDtypeStruct((FB, FF), F32),
            jax.ShapeDtypeStruct((8, 128), F32),
        ),
        in_specs=[
            pl.BlockSpec(memory_space=pltpu.SMEM),
            pl.BlockSpec(memory_space=pltpu.VMEM),
            pl.BlockSpec(memory_space=pltpu.VMEM),
        ],
        out_specs=(
            pl.BlockSpec(memory_space=pltpu.VMEM),
            pl.BlockSpec(memory_space=pltpu.VMEM),
        ),
        scratch_shapes=[pltpu.VMEM((FF, FF), BF16)] * 6 + [pltpu.VMEM((FB, FF), F32)] * 2,
        compiler_params=pltpu.CompilerParams(vmem_limit_bytes=40 * 1024 * 1024),
    )(damp, packed, weight)


def exchange(value, axis):
    return lax.all_to_all(value, axis, split_axis=0, concat_axis=0, tiled=True)


def gather(value, axis, count):
    return exchange(jnp.broadcast_to(value[None], (count,) + value.shape), axis)


def shards(grads, block_expert, grad_weight, damping):
    token_count = grads.shape[0]
    block_total = block_expert.shape[0]
    block_rows = token_count // block_total
    expert_total = 16
    scale = expert_total / (token_count * 512.0)

    same_expert = block_expert[:, None] == block_expert[None, :]
    position = jnp.arange(block_total, dtype=jnp.int32)
    earlier = position[None, :] < position[:, None]
    rank = jnp.sum(jnp.where(same_expert & earlier, 1, 0), axis=1).astype(jnp.int32)
    target = (block_expert % 4) * 4 + block_expert // 4
    slot = target * CAP + rank
    slot_ids = jnp.arange(expert_total * CAP, dtype=jnp.int32)
    placement = (slot_ids[:, None] == slot[None, :]).astype(BF16)
    flat = grads.reshape(block_total, block_rows * FF)
    routed = jnp.dot(placement, flat, preferred_element_type=F32).astype(BF16)
    routed = exchange(routed.reshape(expert_total, CAP * block_rows, FF), ("x", "y"))
    tokens = routed.reshape(-1, FF)
    gram = lax.dot_general(tokens, tokens, (((0,), (0,)), ((), ())), preferred_element_type=F32)

    blocks = [
        gram[i * FB:(i + 1) * FB, j * FB:(j + 1) * FB] for i in range(NB) for j in range(i + 1)
    ]
    packed = jnp.concatenate(blocks + [jnp.zeros((ROWS - TRI * FB, FB), F32)], axis=0)
    packed = packed.reshape(32, 2, CHUNK, FB).transpose(1, 0, 2, 3)
    packed = jnp.sum(exchange(packed, "core"), axis=0)
    packed = exchange(packed, ("x", "zl")).reshape(4, 8, CHUNK, FB).sum(1)
    packed = exchange(packed, ("zh", "core")).reshape(2, 2 * CHUNK, FB).sum(0)
    packed = gather(packed, "zl", 8).reshape(16 * CHUNK, FB)
    packed = gather(packed, "x", 4).reshape(ROWS, FB)

    weight = grad_weight[0]
    result, bad = refined_apply(packed, weight, scale, damping)

    def keep(_):
        return result

    def direct(_):
        return direct_apply(packed[:TRI * FB].reshape(TRI, FB, FB), weight, scale, damping[0])

    return lax.cond(bad[0, 0] == 0.0, keep, direct, 0)[None]


def solution(mesh):
    fine = Mesh(mesh.devices.reshape(4, 8, 4, 2, 2), ("x", "zl", "y", "zh", "core"))
    every = ("x", "zl", "y", "zh", "core")
    return jax.shard_map(
        shards,
        mesh=fine,
        in_specs=(
            P(every, None),
            P(every),
            P(("y", "zh", "core"), ("x", "zl"), None),
            P(("y", "zh", "core")),
        ),
        out_specs=P(("y", "zh", "core"), ("x", "zl"), None),
        check_vma=False,
    )
```

```python
import functools

import jax
import jax.numpy as jnp
from jax import lax
from jax.experimental import pallas as pl
from jax.experimental.pallas import tpu as pltpu
from jax.sharding import Mesh
from jax.sharding import PartitionSpec as P

FB = 128
FF = 768
NB = FF // FB
TRI = NB * (NB + 1) // 2
CAP = 2
TB = 32
EXPERTS = 16
PIECE = TRI * FB // 32
BF16 = jnp.bfloat16
F32 = jnp.float32


def tri_index(row_block, col_block):
    return row_block * (row_block + 1) // 2 + col_block


def dot32(left, right):
    return jnp.dot(left, right, preferred_element_type=F32)


def split(value):
    high = value.astype(BF16)
    return high, (value - high.astype(F32)).astype(BF16)


def solve_kernel(scale, damp_ref, packed_ref, weight_ref, out_ref,
                 fh, fl, r1, r2, r4, r8, bvec, xvec, full):
    damp = damp_ref[0]
    row_id = lax.broadcasted_iota(jnp.int32, (FB, FB), 0)
    col_id = lax.broadcasted_iota(jnp.int32, (FB, FB), 1)
    eye = jnp.where(row_id == col_id, 1.0, 0.0).astype(F32)

    s_row, s_col = [], []
    for i in range(NB):
        t = tri_index(i, i)
        dia = packed_ref[t * FB:(t + 1) * FB, :] * eye
        s_row.append(lax.rsqrt(jnp.sum(dia, axis=0, keepdims=True) * scale + damp))
        s_col.append(lax.rsqrt(jnp.sum(dia, axis=1, keepdims=True) * scale + damp))
    norm = jnp.zeros((FB, FB), F32)
    for i in range(NB):
        for j in range(i + 1):
            t = tri_index(i, j)
            block = packed_ref[t * FB:(t + 1) * FB, :] * scale
            if i == j:
                block = block + damp * eye
            block = block * s_col[i] * s_row[j]
            norm = norm + block * block * (1.0 if i == j else 2.0)
            high, low = split(block)
            fh[i * FB:(i + 1) * FB, j * FB:(j + 1) * FB] = high
            fl[i * FB:(i + 1) * FB, j * FB:(j + 1) * FB] = low
            if i != j:
                turned = block.T
                high, low = split(turned)
                fh[j * FB:(j + 1) * FB, i * FB:(i + 1) * FB] = high
                fl[j * FB:(j + 1) * FB, i * FB:(i + 1) * FB] = low
    total = jnp.sum(jnp.sum(norm, axis=0, keepdims=True), axis=1, keepdims=True)
    alpha = float(FF) / total
    for i in range(NB):
        rows = slice(i * FB, (i + 1) * FB)
        for j in range(NB):
            cols = slice(j * FB, (j + 1) * FB)
            part = fh[rows, cols].astype(F32) + fl[rows, cols].astype(F32)
            value = -alpha * part
            if i == j:
                value = value + eye
            r1[rows, cols] = value.astype(BF16)
    for i in range(NB):
        rows = slice(i * FB, (i + 1) * FB)
        r2[rows, :] = dot32(r1[rows, :], r1[...]).astype(BF16)
    for i in range(NB):
        rows = slice(i * FB, (i + 1) * FB)
        r4[rows, :] = dot32(r2[rows, :], r2[...]).astype(BF16)
    power = jnp.zeros((1, FF), F32)
    for i in range(NB):
        rows = slice(i * FB, (i + 1) * FB)
        value = dot32(r4[rows, :], r4[...])
        power = power + jnp.sum(value * value, axis=0, keepdims=True)
        r8[rows, :] = value.astype(BF16)
    power = jnp.sum(power, axis=1, keepdims=True)

    scales = jnp.concatenate(s_row, axis=1)
    bvec[...] = weight_ref[...].astype(F32) * scales

    def near_inverse(value):
        value = value + dot32(value.astype(BF16), r8[...])
        value = value + dot32(value.astype(BF16), r4[...])
        value = value + dot32(value.astype(BF16), r2[...])
        value = value + dot32(value.astype(BF16), r1[...])
        return value * alpha

    def residual(value):
        high, low = split(value)
        return bvec[...] - (
            dot32(high, fh[...]) + (dot32(low, fh[...]) + dot32(high, fl[...]))
        )

    xvec[...] = near_inverse(bvec[...])
    xvec[...] = xvec[...] + near_inverse(residual(xvec[...]))
    left = residual(xvec[...])
    left_norm = jnp.sum(left * left, axis=1, keepdims=True)
    b_norm = jnp.sum(bvec[...] * bvec[...], axis=1, keepdims=True)
    out_ref[...] = (xvec[...] + near_inverse(left)) * scales
    bad = jnp.sum(jnp.where(left_norm <= 1e-6 * b_norm, 0.0, 1.0), axis=0, keepdims=True)
    bad = bad + jnp.where(power <= 0.25, 0.0, 1.0)

    @pl.when(bad[0, 0] > 0.0)
    def _():
        direct_inverse(scale, damp, packed_ref, s_row, s_col, eye, full)
        out_ref[...] = (
            jnp.dot(bvec[...], full[...], preferred_element_type=F32, precision=lax.Precision.HIGHEST)
            * scales
        )


def direct_inverse(scale, damp, packed_ref, s_row, s_col, eye, full):
    for i in range(NB):
        for j in range(i + 1):
            t = tri_index(i, j)
            block = packed_ref[t * FB:(t + 1) * FB, :] * scale
            if i == j:
                block = block + damp * eye
            block = block * s_col[i] * s_row[j]
            full[i * FB:(i + 1) * FB, j * FB:(j + 1) * FB] = block
            if i != j:
                full[j * FB:(j + 1) * FB, i * FB:(i + 1) * FB] = block.T
    lanes = lax.broadcasted_iota(jnp.int32, (1, FF), 1)
    sublanes = lax.broadcasted_iota(jnp.int32, (FB, 1), 0)

    def step(k, carry):
        at = jnp.where(lanes == k, 1.0, 0.0)
        row = full[pl.ds(k, 1), :]
        inv = 1.0 / jnp.sum(row * at, axis=1, keepdims=True)
        scaled = row * inv
        scaled = jnp.where(lanes == k, inv, scaled)

        def part(i, inner):
            start = pl.multiple_of(i * FB, FB)
            own = full[pl.ds(start, FB), :]
            column = jnp.sum(own * at, axis=1, keepdims=True)
            rest = own * (1.0 - at) - column * scaled
            full[pl.ds(start, FB), :] = jnp.where(sublanes + start == k, scaled, rest)
            return inner

        return lax.fori_loop(0, NB, part, carry)

    lax.fori_loop(0, FF, step, 0)


def refined_apply(packed, weight, scale, damp):
    return pl.pallas_call(
        functools.partial(solve_kernel, scale),
        out_shape=jax.ShapeDtypeStruct((FB, FF), F32),
        in_specs=[
            pl.BlockSpec(memory_space=pltpu.SMEM),
            pl.BlockSpec(memory_space=pltpu.VMEM),
            pl.BlockSpec(memory_space=pltpu.VMEM),
        ],
        out_specs=pl.BlockSpec(memory_space=pltpu.VMEM),
        scratch_shapes=[pltpu.VMEM((FF, FF), BF16)] * 6
        + [pltpu.VMEM((FB, FF), F32)] * 2
        + [pltpu.VMEM((FF, FF), F32)],
        compiler_params=pltpu.CompilerParams(vmem_limit_bytes=40 * 1024 * 1024),
    )(damp, packed, weight)


def exchange(value, axis):
    return lax.all_to_all(value, axis, split_axis=0, concat_axis=0, tiled=True)


def gather(value, axis, count):
    return exchange(jnp.broadcast_to(value[None], (count,) + value.shape), axis)


def route_kernel(expert_ref, grads_ref, out_ref, seen):
    for e in range(EXPERTS):
        seen[e] = 0
    out_ref[...] = jnp.zeros_like(out_ref)
    for b in range(grads_ref.shape[0] // TB):
        expert = expert_ref[b]
        rank = seen[expert]
        seen[expert] = rank + 1
        target = (expert % 4) * 4 + expert // 4
        start = pl.multiple_of((target * CAP + rank) * TB, TB)
        out_ref[pl.ds(start, TB), :] = grads_ref[b * TB:(b + 1) * TB, :]


def route(grads, block_expert):
    return pl.pallas_call(
        route_kernel,
        out_shape=jax.ShapeDtypeStruct((EXPERTS * CAP * TB, FF), BF16),
        in_specs=[
            pl.BlockSpec(memory_space=pltpu.SMEM),
            pl.BlockSpec(memory_space=pltpu.VMEM),
        ],
        out_specs=pl.BlockSpec(memory_space=pltpu.VMEM),
        scratch_shapes=[pltpu.SMEM((EXPERTS,), jnp.int32)],
        compiler_params=pltpu.CompilerParams(vmem_limit_bytes=16 * 1024 * 1024),
    )(block_expert, grads)


def shards(grads, block_expert, grad_weight, damping):
    scale = EXPERTS / (grads.shape[0] * 512.0)
    routed = route(grads, block_expert).reshape(EXPERTS, CAP * TB, FF)
    tokens = exchange(routed, ("x", "y")).reshape(-1, FF)
    gram = lax.dot_general(tokens, tokens, (((0,), (0,)), ((), ())), preferred_element_type=F32)

    blocks = [
        gram[i * FB:(i + 1) * FB, j * FB:(j + 1) * FB] for i in range(NB) for j in range(i + 1)
    ]
    packed = jnp.concatenate(blocks, axis=0)
    packed = packed.reshape(16, 2, PIECE, FB).transpose(1, 0, 2, 3)
    packed = jnp.sum(exchange(packed, "core"), axis=0)
    packed = exchange(packed, ("x", "zb")).reshape(4, 4, PIECE, FB).sum(1)
    packed = jnp.broadcast_to(packed[None], (2, 4, PIECE, FB)).reshape(8, PIECE, FB)
    packed = exchange(packed, ("za", "zh", "core")).reshape(4, 2 * PIECE, FB).sum(0)
    packed = gather(packed, "zb", 4).reshape(8 * PIECE, FB)
    packed = gather(packed, "x", 4).reshape(32 * PIECE, FB)
    return refined_apply(packed, grad_weight[0], scale, damping)[None]


def solution(mesh):
    every = ("x", "za", "zb", "y", "zh", "core")
    fine = Mesh(mesh.devices.reshape(4, 2, 4, 4, 2, 2), every)
    experts, rows = ("y", "zh", "core"), ("x", "za", "zb")
    return jax.shard_map(
        shards,
        mesh=fine,
        in_specs=(P(every, None), P(every), P(experts, rows, None), P(experts)),
        out_specs=P(experts, rows, None),
        check_vma=False,
    )
```
